256 devices in a mesh: row: 32 (over y, x, core), col: 8 (over z).
Axes of the slice: x: 4, y: 4, z: 8, core: 2. Of those that a mesh axis runs over, the one named last changes fastest.
Arguments:
- matrix: float32 [4, 8192, 4, 2048], P(None, 'row', None, 'col'), may hold values from -12 to 16, as said below
Outputs:
- factored: float32 [4, 8192, 4, 2048], P(None, 'row', None, 'col')
The draws below stay inside these ranges and needn't reach their ends.
Inputs may be any that keep to these rules, and one draw needn't show every extreme that they name: `matrix`: the leading block of order 2 * 256 is symmetric and positive definite, with all its eigenvalues 4 or more; every other diagonal entry lies between 12 and 16.
All inputs are finite; a program needn't handle non-finite values.
Results may differ from the reference program's by a relative error of at most 0.0001.
Values sent between devices are 32-bit elements; how exact they have to be, the bound alone decides.
No kernel may reach another device: no remote copies, remote signals or barrier semaphores. Data moves between devices by JAX's collectives and lax.ppermute only.
A program may use at most 128 MiB of HBM per device.

```python
import jax
import jax.numpy as jnp
from jax import lax

TB = 256
RT = 4
CT = 4
ORDER = 32768
SLAB = 8192
N_ROW = 32
N_COL = 8


def draw_matrix(key, part):
    key = jax.random.fold_in(key, 7)
    key_off, key_lead, key_diag = jax.random.split(key, 3)
    shape = (RT, TB * N_ROW, CT, TB * N_COL)
    width = 2 * TB
    rows = lax.broadcasted_iota(jnp.int32, shape, 0) * (TB * N_ROW) + lax.broadcasted_iota(jnp.int32, shape, 1)
    cols = lax.broadcasted_iota(jnp.int32, shape, 2) * (TB * N_COL) + lax.broadcasted_iota(jnp.int32, shape, 3)
    outer = 0.35 * jnp.clip(jax.random.normal(key_off, shape, jnp.float32), -6.0, 6.0)
    factors = jnp.clip(jax.random.normal(key_lead, (width, width), jnp.float32), -1.7, 1.7)
    product = jnp.dot(factors, factors.T, precision=lax.Precision.HIGHEST, preferred_element_type=jnp.float32)
    leading = 4.0 * (0.5 * (product + product.T) / width + jnp.eye(width, dtype=jnp.float32))
    spread = jax.random.uniform(key_diag, shape, jnp.float32, 0.0, 1.0)
    base = jnp.where(rows == cols, 12.0 + 4.0 * spread, outer)
    base = base.at[0, :width, 0, :width].set(leading)
    return base.astype(jnp.float32)


def setup_inputs(seed: int = 0) -> dict:
    seeds = jax.random.split(jax.random.key(seed), 2)
    return {
        "matrix": draw_matrix(jax.random.fold_in(seeds[1], 71), 0),
    }


def reference(matrix):
    whole = matrix.reshape(ORDER, SLAB)
    eye = jnp.eye(TB, dtype=jnp.float32)
    for k in range(2):
        s = k * TB
        corner = whole[s:s + TB, s:s + TB]
        lower = jnp.linalg.cholesky(corner)
        inverse = lax.linalg.triangular_solve(lower, eye, left_side=True, lower=True)
        below = jnp.dot(whole[s + TB:, s:s + TB].astype(jnp.float32), inverse.T.astype(jnp.float32), precision=lax.Precision.HIGHEST, preferred_element_type=jnp.float32)
        column = jnp.concatenate([jnp.zeros((s, TB), jnp.float32), lower, below], axis=0)
        whole = whole.at[:, s:s + TB].set(column)
        update = jnp.dot(below.astype(jnp.float32), below[:SLAB - s - TB].T.astype(jnp.float32), precision=lax.Precision.HIGHEST, preferred_element_type=jnp.float32)
        whole = whole.at[s + TB:, s + TB:].add(-update)
    return whole.reshape(RT, TB * N_ROW, CT, TB * N_COL)
```

```python
import jax
import jax.numpy as jnp
from jax import lax
from jax.experimental import pallas as pl
from jax.experimental.pallas import tpu as pltpu
from jax.sharding import PartitionSpec as P

HI = lax.Precision.HIGHEST
F32 = jnp.float32
BF16 = jnp.bfloat16
B = 128
T = 256
MIB = 1024 * 1024


def dot(a, b):
    return lax.dot_general(a, b, (((1,), (0,)), ((), ())), precision=HI, preferred_element_type=F32)


def dot_t(a, b):
    return lax.dot_general(a, b, (((1,), (1,)), ((), ())), precision=HI, preferred_element_type=F32)


def leaf(d):
    n = d.shape[0]
    sub = lax.broadcasted_iota(jnp.int32, (8, B), 0)
    row = lax.broadcasted_iota(jnp.int32, (n, B), 0)
    col = lax.broadcasted_iota(jnp.int32, (n, B), 1)
    e = jnp.where(row == col, 1.0, 0.0).astype(F32)
    out = []
    for q in range(n // 8):
        left = n - 8 * q
        rest = left - 8
        cols = [jnp.broadcast_to(d[:, 8 * q + k : 8 * q + k + 1], (left, B)) for k in range(8)]
        tops, lows = [], []
        scale = jnp.zeros((8, B), F32)
        for k in range(8):
            pivot = jnp.broadcast_to(cols[k][k : k + 1, :], (8, B))
            reciprocal = 1.0 / pivot
            scale = jnp.where(sub == k, lax.rsqrt(pivot), scale)
            top = jnp.where(sub > k, cols[k][:8] * reciprocal, 0.0)
            tops.append(top)
            if rest:
                low = cols[k][8:] * jnp.broadcast_to(reciprocal[:1], (rest, B))
                lows.append(low)
            for l in range(k + 1, 8):
                u = cols[l][k : k + 1, :]
                t = cols[l][:8] - top * jnp.broadcast_to(u, (8, B))
                if rest:
                    r = cols[l][8:] - low * jnp.broadcast_to(u, (rest, B))
                    t = jnp.concatenate([t, r], 0)
                cols[l] = t
        d_top, e_top = d[:8], e[:8]
        d_rows, e_rows = [], []
        for k in range(8):
            a, b = d_top[k : k + 1, :], e_top[k : k + 1, :]
            d_rows.append(a)
            e_rows.append(b)
            d_top = d_top - tops[k] * jnp.broadcast_to(a, (8, B))
            e_top = e_top - tops[k] * jnp.broadcast_to(b, (8, B))
        out.append(e_top * scale)
        if rest:
            d, e = d[8:], e[8:]
            for k in range(8):
                d = d - lows[k] * jnp.broadcast_to(d_rows[k], (rest, B))
                e = e - lows[k] * jnp.broadcast_to(e_rows[k], (rest, B))
    return jnp.concatenate(out, 0)


def factor_kernel(s00, s10, s11, w, a, e):
    a[0:T, 0:T] = 0.5 * (s00[...] + s00[...].T)
    a[T:, 0:T] = s10[...]
    a[T:, T:] = 0.5 * (s11[...] + s11[...].T)
    w[...] = jnp.zeros_like(w)
    e[...] = jnp.zeros_like(e)
    for i in range(4):
        o = i * B
        p = o + B
        part = leaf(a[o:p, o:p])
        w[o:p, o:p] = part
        if i:
            w[o:p, 0:o] = dot(part, e[o:p, 0:o])
        if i < 3:
            low = dot_t(a[p:, o:p], part)
            for j in range(i + 1, 4):
                r = (j - i - 1) * B
                a[j * B :, j * B : (j + 1) * B] -= dot_t(low[r:], low[r : r + B])
            e[p:, 0:p] -= dot(low, w[o:p, 0:p])


def factor(s00, s10, s11):
    vmem = pl.BlockSpec(memory_space=pltpu.VMEM)
    return pl.pallas_call(
        factor_kernel,
        out_shape=jax.ShapeDtypeStruct((2 * T, 2 * T), F32),
        in_specs=[vmem] * 3,
        out_specs=vmem,
        scratch_shapes=[pltpu.VMEM((2 * T, 2 * T), F32)] * 2,
        compiler_params=pltpu.CompilerParams(vmem_limit_bytes=16 * MIB),
        cost_estimate=pl.CostEstimate(flops=10**9, bytes_accessed=2 * MIB, transcendentals=0),
    )(s00, s10, s11)


def split(x):
    high = x.astype(BF16)
    return high, (x - high.astype(F32)).astype(BF16)


def update_kernel(where, a, p, g0, g1, g2, g3, h0, h1, h2, h3, w, out, mirror, y_high, y_low):
    r, c = where[0], where[1]
    m = pl.program_id(0)
    core = lax.rem(r, 2)
    y = r // 8

    def solve(first, second):
        x0 = dot_t(first, w[0:T, 0:T])
        x1 = dot_t(first, w[T:, 0:T]) + dot_t(second, w[T:, T:])
        return x0, x1

    @pl.when(m == 0)
    def _():
        for s, (g, h) in enumerate(((g0, h0), (g1, h1), (g2, h2), (g3, h3))):
            n = lax.rem(y - s + 4, 4)
            mirror[core, n] = g[...]
            mirror[1 - core, n] = h[...]
        for n in range(4):
            x0, x1 = solve(mirror[0, n], mirror[1, n])
            tile = n * 8 + c
            x0 = jnp.where(tile > 0, x0, 0.0)
            x1 = jnp.where(tile > 1, x1, 0.0)
            for k, x in enumerate((x0, x1)):
                high, low = split(x)
                y_high[n * T : (n + 1) * T, k * T : (k + 1) * T] = high
                y_low[n * T : (n + 1) * T, k * T : (k + 1) * T] = low

    x0, x1 = solve(p[:, 0].reshape(T, T), p[:, 1].reshape(T, T))
    tile = m * 32 + r
    u0 = jnp.where(tile > 0, x0, 0.0)
    u1 = jnp.where(tile > 1, x1, 0.0)
    x_high, x_low = split(jnp.concatenate([u0, u1], axis=1))

    def mul(u, v):
        return lax.dot_general(u, v, (((1,), (1,)), ((), ())), preferred_element_type=F32)

    for n in range(4):
        span = slice(n * T, (n + 1) * T)
        product = mul(x_high, y_high[span]) + mul(x_high, y_low[span]) + mul(x_low, y_high[span])
        for half in range(2):
            at = pl.ds(half * 4 + n, T, stride=8)
            out[at, :] = a[at, :] - product[:, half * B : (half + 1) * B]

    @pl.when(c < 2)
    def _():
        row = lax.broadcasted_iota(jnp.int32, (T, T), 0)
        col = lax.broadcasted_iota(jnp.int32, (T, T), 1)
        x = jnp.where(c == 0, x0, x1)
        keep = (tile > c) | ((tile == c) & (row >= col))
        x = jnp.where(keep, x, 0.0)
        for half in range(2):
            out[pl.ds(half * 4, T, stride=8), :] = x[:, half * B : (half + 1) * B]


def update(where, a, p, g, h, w):
    whole = pl.BlockSpec((T, T), lambda m: (0, 0))
    return pl.pallas_call(
        update_kernel,
        grid=(4,),
        out_shape=jax.ShapeDtypeStruct(a.shape, F32),
        in_specs=[
            pl.BlockSpec(memory_space=pltpu.SMEM),
            pl.BlockSpec((8 * T, B), lambda m: (m, 0)),
            pl.BlockSpec((2, 2, B, T), lambda m: (m, 0, 0, 0)),
        ]
        + [whole] * 8
        + [pl.BlockSpec((2 * T, 2 * T), lambda m: (0, 0))],
        out_specs=pl.BlockSpec((8 * T, B), lambda m: (m, 0)),
        scratch_shapes=[
            pltpu.VMEM((2, 4, T, T), F32),
            pltpu.VMEM((4 * T, 2 * T), BF16),
            pltpu.VMEM((4 * T, 2 * T), BF16),
        ],
        compiler_params=pltpu.CompilerParams(vmem_limit_bytes=32 * MIB),
        cost_estimate=pl.CostEstimate(flops=8 * 10**9, bytes_accessed=12 * MIB, transcendentals=0),
    )(where, a, p, *g, *h, w)


def device(r, c):
    return r * 8 + c


def send(x, pairs):
    return lax.ppermute(x, ("row", "col"), [(device(*a), device(*b)) for a, b in pairs])


def total(x, parts):
    for part in parts:
        x = x + part
    return x


def broadcast(x):
    x = total(x, [send(x, [((0, 0), (8 * s, 0))]) for s in (1, 2, 3)])
    x = total(x, [send(x, [((8 * y, 0), (8 * y + 2 * s, 0)) for y in range(4)]) for s in (1, 2, 3)])
    chips = range(0, 32, 2)
    x = total(x, [send(x, [((r, 0), (r, 2 * s)) for r in chips]) for s in (1, 2, 3)])
    x = total(x, [send(x, [((r, z), (r, z + 1)) for r in chips for z in range(0, 8, 2)])])
    return total(x, [send(x, [((r, z), (r + 1, z)) for r in chips for z in range(8)])])


def per_device(matrix):
    r = lax.axis_index("row")
    c = lax.axis_index("col")
    flat = matrix.reshape(4, T, 4, 2, B).transpose(0, 1, 3, 2, 4).reshape(4 * T * 8, B)
    column = matrix[:, :, 0, :]

    first = column[0]
    origin = (r == 0) & (c == 0)
    s00 = broadcast(jnp.where(origin, first, 0.0))
    s10 = send(first, [((1, 0), (0, 0))])
    s11 = send(first, [((1, 1), (0, 0))])
    rest = broadcast(jnp.concatenate([s10, s11], axis=0))

    chunks = column.reshape(8, B, T)
    got = [lax.dynamic_index_in_dim(chunks, c, 0, keepdims=False)]
    for s in range(1, 8):
        piece = lax.dynamic_index_in_dim(chunks, lax.rem(c + s, 8), 0, keepdims=False)
        got.append(lax.ppermute(piece, "col", [(0, s), (1, (1 + s) % 8)]))
    got = jnp.stack(got)
    mine = [lax.dynamic_index_in_dim(got, lax.rem(c + 8 - k, 8), 0, keepdims=False) for k in range(2)]
    panel = lax.all_gather(jnp.stack(mine), "col", axis=0)

    v = send(first, [((i, k), (i // 2 * 2 + k, i % 8)) for i in range(32) for k in range(2)])
    lanes = [(y, z, k) for y in range(4) for z in range(8) for k in range(2)]
    v = total(
        v,
        [
            send(v, [((8 * y + z // 2 * 2 + k, z), (8 * y + (z // 2 + s) % 4 * 2 + k, z)) for y, z, k in lanes])
            for s in (1, 2, 3)
        ],
    )
    g = [v] + [lax.ppermute(v, "row", [(i, (i + 8 * s) % 32) for i in range(32)]) for s in (1, 2, 3)]
    h = [lax.ppermute(t, "row", [(i, i ^ 1) for i in range(32)]) for t in g]

    w = factor(s00, rest[:T], rest[T:])
    where = jnp.stack([r, c]).astype(jnp.int32)
    out = update(where, flat, panel, g, h, w)
    return out.reshape(4, T, 2, 4, B).transpose(0, 1, 3, 2, 4).reshape(4, T, 4, T)


def solution(mesh):
    spec = P(None, "row", None, "col")
    return jax.shard_map(per_device, mesh=mesh, in_specs=(spec,), out_specs=spec, check_vma=False)
```

```python
import jax
import jax.numpy as jnp
from jax import lax
from jax.experimental import pallas as pl
from jax.experimental.pallas import tpu as pltpu
from jax.sharding import PartitionSpec as P

HI = lax.Precision.HIGHEST
F32 = jnp.float32
BF16 = jnp.bfloat16
B = 128
T = 256
MIB = 1024 * 1024


def dot(a, b):
    return lax.dot_general(a, b, (((1,), (0,)), ((), ())), precision=HI, preferred_element_type=F32)


def dot_t(a, b):
    return lax.dot_general(a, b, (((1,), (1,)), ((), ())), precision=HI, preferred_element_type=F32)


def leaf(d):
    n = d.shape[0]
    sub = lax.broadcasted_iota(jnp.int32, (8, B), 0)
    row = lax.broadcasted_iota(jnp.int32, (n, B), 0)
    col = lax.broadcasted_iota(jnp.int32, (n, B), 1)
    e = jnp.where(row == col, 1.0, 0.0).astype(F32)
    out = []
    for q in range(n // 8):
        left = n - 8 * q
        rest = left - 8
        cols = [jnp.broadcast_to(d[:, 8 * q + k : 8 * q + k + 1], (left, B)) for k in range(8)]
        tops, lows = [], []
        scale = jnp.zeros((8, B), F32)
        for k in range(8):
            pivot = jnp.broadcast_to(cols[k][k : k + 1, :], (8, B))
            reciprocal = 1.0 / pivot
            scale = jnp.where(sub == k, lax.rsqrt(pivot), scale)
            top = jnp.where(sub > k, cols[k][:8] * reciprocal, 0.0)
            tops.append(top)
            if rest:
                low = cols[k][8:] * jnp.broadcast_to(reciprocal[:1], (rest, B))
                lows.append(low)
            for l in range(k + 1, 8):
                u = cols[l][k : k + 1, :]
                t = cols[l][:8] - top * jnp.broadcast_to(u, (8, B))
                if rest:
                    r = cols[l][8:] - low * jnp.broadcast_to(u, (rest, B))
                    t = jnp.concatenate([t, r], 0)
                cols[l] = t
        d_top, e_top = d[:8], e[:8]
        d_rows, e_rows = [], []
        for k in range(8):
            a, b = d_top[k : k + 1, :], e_top[k : k + 1, :]
            d_rows.append(a)
            e_rows.append(b)
            d_top = d_top - tops[k] * jnp.broadcast_to(a, (8, B))
            e_top = e_top - tops[k] * jnp.broadcast_to(b, (8, B))
        out.append(e_top * scale)
        if rest:
            d, e = d[8:], e[8:]
            for k in range(8):
                d = d - lows[k] * jnp.broadcast_to(d_rows[k], (rest, B))
                e = e - lows[k] * jnp.broadcast_to(e_rows[k], (rest, B))
    return jnp.concatenate(out, 0)


VMEM = pl.BlockSpec(memory_space=pltpu.VMEM)
SMEM = pl.BlockSpec(memory_space=pltpu.SMEM)
CHIPS = 16
LEAD = 24


def rows_of(chip, core):
    return pl.ds(pl.multiple_of(16 * chip + 8 * core, 8), 8)


def outward_kernel(where, pieces, first, got1, got2, got3, out, share):
    for z in range(8):
        for i, tile in enumerate((z, z + 8, z + 16, z + 24, 0, 1)):
            out[z, 8 * i : 8 * i + 8] = pieces[tile]
    share[...] = jnp.where(where[1] < 2, first[...], got1[...] + got2[...] + got3[...])


def outward(where, pieces, first, got):
    return pl.pallas_call(
        outward_kernel,
        out_shape=[jax.ShapeDtypeStruct((8, 48, T), F32), jax.ShapeDtypeStruct((T, T), F32)],
        in_specs=[SMEM] + [VMEM] * 5,
        out_specs=[VMEM] * 2,
        compiler_params=pltpu.CompilerParams(vmem_limit_bytes=4 * MIB),
        cost_estimate=pl.CostEstimate(flops=0, bytes_accessed=MIB, transcendentals=0),
    )(where, pieces, first, *got)


def inward_kernel(lines, tile, out, share):
    head = jnp.concatenate([lines[0, 32:48], lines[1, 40:48]], axis=0)
    for j in range(CHIPS):
        out[j, 0:LEAD] = head
        out[j, LEAD : LEAD + 32] = lines[0, 0:32]
        out[j, LEAD + 32 :] = lines[1, 0:32]
    share[...] = tile[...]


def inward(lines, tile):
    return pl.pallas_call(
        inward_kernel,
        out_shape=[jax.ShapeDtypeStruct((CHIPS, LEAD + 64, T), F32), jax.ShapeDtypeStruct((T, T), F32)],
        in_specs=[VMEM] * 2,
        out_specs=[VMEM, pl.BlockSpec((T, T), lambda: (0, 0))],
        compiler_params=pltpu.CompilerParams(vmem_limit_bytes=4 * MIB),
        cost_estimate=pl.CostEstimate(flops=0, bytes_accessed=2 * MIB, transcendentals=0),
    )(lines, tile)


def head_kernel(both, lead):
    lead[...] = both[:, 0:LEAD]


def head(both):
    return pl.pallas_call(
        head_kernel,
        out_shape=jax.ShapeDtypeStruct((CHIPS, LEAD, T), F32),
        in_specs=[VMEM],
        out_specs=VMEM,
        compiler_params=pltpu.CompilerParams(vmem_limit_bytes=4 * MIB),
        cost_estimate=pl.CostEstimate(flops=0, bytes_accessed=MIB, transcendentals=0),
    )(both)


def factor_kernel(where, mine, other, w, a, e, tiles):
    core = lax.rem(where[0], 2)
    for j in range(CHIPS):
        for t in range(3):
            tiles[t, rows_of(j, core)] = mine[j, 8 * t : 8 * t + 8]
            tiles[t, rows_of(j, 1 - core)] = other[j, 8 * t : 8 * t + 8]
    a[0:T, 0:T] = 0.5 * (tiles[0] + tiles[0].T)
    a[T:, 0:T] = tiles[1]
    a[T:, T:] = 0.5 * (tiles[2] + tiles[2].T)
    w[...] = jnp.zeros_like(w)
    e[...] = jnp.zeros_like(e)
    for i in range(4):
        o = i * B
        p = o + B
        part = leaf(a[o:p, o:p])
        w[o:p, o:p] = part
        if i:
            w[o:p, 0:o] = dot(part, e[o:p, 0:o])
        if i < 3:
            low = dot_t(a[p:, o:p], part)
            for j in range(i + 1, 4):
                r = (j - i - 1) * B
                a[j * B :, j * B : (j + 1) * B] -= dot_t(low[r:], low[r : r + B])
            e[p:, 0:p] -= dot(low, w[o:p, 0:p])


def factor(where, mine, other):
    return pl.pallas_call(
        factor_kernel,
        out_shape=jax.ShapeDtypeStruct((2 * T, 2 * T), F32),
        in_specs=[SMEM, VMEM, VMEM],
        out_specs=VMEM,
        scratch_shapes=[pltpu.VMEM((2 * T, 2 * T), F32)] * 2 + [pltpu.VMEM((3, T, T), F32)],
        compiler_params=pltpu.CompilerParams(vmem_limit_bytes=12 * MIB),
        cost_estimate=pl.CostEstimate(flops=10**9, bytes_accessed=60 * MIB, transcendentals=0),
    )(where, mine, other)


def split(x):
    high = x.astype(BF16)
    return high, (x - high.astype(F32)).astype(BF16)


def update_kernel(where, a, p0, p1, mine, other, w, out, mirror, y_high, y_low):
    r, c = where[0], where[1]
    m = pl.program_id(0)
    core = lax.rem(r, 2)

    def solve(first, second):
        x0 = dot_t(first, w[0:T, 0:T])
        x1 = dot_t(first, w[T:, 0:T]) + dot_t(second, w[T:, T:])
        return x0, x1

    @pl.when(m == 0)
    def _():
        for j in range(CHIPS):
            for k in range(2):
                for n in range(4):
                    at = LEAD + 32 * k + 8 * n
                    mirror[k, n, rows_of(j, core)] = mine[j, at : at + 8]
                    mirror[k, n, rows_of(j, 1 - core)] = other[j, at : at + 8]
        for n in range(4):
            x0, x1 = solve(mirror[0, n], mirror[1, n])
            tile = n * 8 + c
            x0 = jnp.where(tile > 0, x0, 0.0)
            x1 = jnp.where(tile > 1, x1, 0.0)
            for k, x in enumerate((x0, x1)):
                high, low = split(x)
                y_high[n * T : (n + 1) * T, k * T : (k + 1) * T] = high
                y_low[n * T : (n + 1) * T, k * T : (k + 1) * T] = low

    x0, x1 = solve(p0[0], p1[0])
    tile = m * 32 + r
    u0 = jnp.where(tile > 0, x0, 0.0)
    u1 = jnp.where(tile > 1, x1, 0.0)
    x_high, x_low = split(jnp.concatenate([u0, u1], axis=1))

    def mul(u, v):
        return lax.dot_general(u, v, (((1,), (1,)), ((), ())), preferred_element_type=F32)

    for n in range(4):
        span = slice(n * T, (n + 1) * T)
        product = mul(x_high, y_high[span]) + mul(x_high, y_low[span]) + mul(x_low, y_high[span])
        for half in range(2):
            at = pl.ds(half * 4 + n, T, stride=8)
            out[at, :] = a[at, :] - product[:, half * B : (half + 1) * B]

    @pl.when(c < 2)
    def _():
        row = lax.broadcasted_iota(jnp.int32, (T, T), 0)
        col = lax.broadcasted_iota(jnp.int32, (T, T), 1)
        x = jnp.where(c == 0, x0, x1)
        keep = (tile > c) | ((tile == c) & (row >= col))
        x = jnp.where(keep, x, 0.0)
        for half in range(2):
            out[pl.ds(half * 4, T, stride=8), :] = x[:, half * B : (half + 1) * B]


def update(where, a, panel, mine, other, w):
    return pl.pallas_call(
        update_kernel,
        grid=(4,),
        out_shape=jax.ShapeDtypeStruct(a.shape, F32),
        in_specs=[
            SMEM,
            pl.BlockSpec((8 * T, B), lambda m: (m, 0)),
            pl.BlockSpec((1, T, T), lambda m: (lax.rem(8 - m, 8), 0, 0)),
            pl.BlockSpec((1, T, T), lambda m: (1 + m, 0, 0)),
        ]
        + [VMEM] * 3,
        out_specs=pl.BlockSpec((8 * T, B), lambda m: (m, 0)),
        scratch_shapes=[
            pltpu.VMEM((2, 4, T, T), F32),
            pltpu.VMEM((4 * T, 2 * T), BF16),
            pltpu.VMEM((4 * T, 2 * T), BF16),
        ],
        compiler_params=pltpu.CompilerParams(vmem_limit_bytes=52 * MIB),
        cost_estimate=pl.CostEstimate(flops=8 * 10**9, bytes_accessed=12 * MIB, transcendentals=0),
    )(where, a, panel, panel, mine, other, w)


def per_device(matrix):
    r = lax.axis_index("row")
    c = lax.axis_index("col")
    where = jnp.stack([r, c]).astype(jnp.int32)
    flat = matrix.reshape(4, T, 4, 2, B).transpose(0, 1, 3, 2, 4).reshape(4 * T * 8, B)
    column = matrix[:, :, 0, :]
    first = column[0]

    got = [lax.ppermute(column[m], "col", [(0, 8 - m), (1, 1 + m)]) for m in (1, 2, 3)]
    pieces = lax.all_to_all(first.reshape(32, 8, T), "row", 0, 0)
    spread, tile = outward(where, pieces, first, got)
    both, share = inward(lax.all_to_all(spread, "col", 0, 0), tile)
    panel = lax.all_gather(share, "col", axis=0)

    cores = [[2 * j + k for j in range(CHIPS)] for k in range(2)]
    both = lax.all_to_all(both, "row", 0, 0, axis_index_groups=cores)
    swap = [(i, i ^ 1) for i in range(32)]
    w = factor(where, both, lax.ppermute(head(both), "row", swap))
    out = update(where, flat, panel, both, lax.ppermute(both, "row", swap), w)
    return out.reshape(4, T, 2, 4, B).transpose(0, 1, 3, 2, 4).reshape(4, T, 4, T)


def solution(mesh):
    spec = P(None, "row", None, "col")
    return jax.shard_map(per_device, mesh=mesh, in_specs=(spec,), out_specs=spec, check_vma=False)
```

```python
import jax
import jax.numpy as jnp
from jax import lax
from jax.experimental import pallas as pl
from jax.experimental.pallas import tpu as pltpu
from jax.sharding import PartitionSpec as P

HI = lax.Precision.HIGHEST
F32 = jnp.float32
BF16 = jnp.bfloat16
B = 128
T = 256
MIB = 1024 * 1024


def dot(a, b):
    return lax.dot_general(a, b, (((1,), (0,)), ((), ())), precision=HI, preferred_element_type=F32)


def dot_t(a, b):
    return lax.dot_general(a, b, (((1,), (1,)), ((), ())), precision=HI, preferred_element_type=F32)


def leaf(d):
    n = d.shape[0]
    sub = lax.broadcasted_iota(jnp.int32, (8, B), 0)
    row = lax.broadcasted_iota(jnp.int32, (n, B), 0)
    col = lax.broadcasted_iota(jnp.int32, (n, B), 1)
    e = jnp.where(row == col, 1.0, 0.0).astype(F32)
    out = []
    for q in range(n // 8):
        left = n - 8 * q
        rest = left - 8
        cols = [jnp.broadcast_to(d[:, 8 * q + k : 8 * q + k + 1], (left, B)) for k in range(8)]
        tops, lows = [], []
        scale = jnp.zeros((8, B), F32)
        for k in range(8):
            pivot = jnp.broadcast_to(cols[k][k : k + 1, :], (8, B))
            reciprocal = 1.0 / pivot
            scale = jnp.where(sub == k, lax.rsqrt(pivot), scale)
            top = jnp.where(sub > k, cols[k][:8] * reciprocal, 0.0)
            tops.append(top)
            if rest:
                low = cols[k][8:] * jnp.broadcast_to(reciprocal[:1], (rest, B))
                lows.append(low)
            for l in range(k + 1, 8):
                u = cols[l][k : k + 1, :]
                t = cols[l][:8] - top * jnp.broadcast_to(u, (8, B))
                if rest:
                    r = cols[l][8:] - low * jnp.broadcast_to(u, (rest, B))
                    t = jnp.concatenate([t, r], 0)
                cols[l] = t
        d_top, e_top = d[:8], e[:8]
        d_rows, e_rows = [], []
        for k in range(8):
            a, b = d_top[k : k + 1, :], e_top[k : k + 1, :]
            d_rows.append(a)
            e_rows.append(b)
            d_top = d_top - tops[k] * jnp.broadcast_to(a, (8, B))
            e_top = e_top - tops[k] * jnp.broadcast_to(b, (8, B))
        out.append(e_top * scale)
        if rest:
            d, e = d[8:], e[8:]
            for k in range(8):
                d = d - lows[k] * jnp.broadcast_to(d_rows[k], (rest, B))
                e = e - lows[k] * jnp.broadcast_to(e_rows[k], (rest, B))
    return jnp.concatenate(out, 0)


VMEM = pl.BlockSpec(memory_space=pltpu.VMEM)
SMEM = pl.BlockSpec(memory_space=pltpu.SMEM)
CHIPS = 16
LEAD = 24


def rows_of(chip, core):
    return pl.ds(pl.multiple_of(16 * chip + 8 * core, 8), 8)


def outward_kernel(where, pieces, first, got1, got2, got3, out, share):
    for z in range(8):
        for i, tile in enumerate((z, z + 8, z + 16, z + 24, 0, 1)):
            out[z, 8 * i : 8 * i + 8] = pieces[tile]
    share[...] = jnp.where(where[1] < 2, first[...], got1[...] + got2[...] + got3[...])


def outward(where, pieces, first, got):
    return pl.pallas_call(
        outward_kernel,
        out_shape=[jax.ShapeDtypeStruct((8, 48, T), F32), jax.ShapeDtypeStruct((T, T), F32)],
        in_specs=[SMEM] + [VMEM] * 5,
        out_specs=[VMEM] * 2,
        compiler_params=pltpu.CompilerParams(vmem_limit_bytes=4 * MIB),
        cost_estimate=pl.CostEstimate(flops=0, bytes_accessed=MIB, transcendentals=0),
    )(where, pieces, first, *got)


def inward_kernel(lines, tile, out, share):
    for j in range(CHIPS):
        out[j, 0:16] = lines[0, 32:48]
        out[j, 16:LEAD] = lines[1, 40:48]
        out[j, LEAD : LEAD + 32] = lines[0, 0:32]
        out[j, LEAD + 32 :] = lines[1, 0:32]
    share[...] = tile[...]


def inward(lines, tile):
    return pl.pallas_call(
        inward_kernel,
        out_shape=[jax.ShapeDtypeStruct((CHIPS, LEAD + 64, T), F32), square(T)],
        in_specs=[VMEM] * 2,
        out_specs=[VMEM, pl.BlockSpec((T, T), lambda: (0, 0))],
        compiler_params=pltpu.CompilerParams(vmem_limit_bytes=4 * MIB),
        cost_estimate=pl.CostEstimate(flops=0, bytes_accessed=2 * MIB, transcendentals=0),
    )(lines, tile)


def head_kernel(both, lead):
    lead[...] = both[:, 0:LEAD]


def head(both):
    return pl.pallas_call(
        head_kernel,
        out_shape=jax.ShapeDtypeStruct((CHIPS, LEAD, T), F32),
        in_specs=[VMEM],
        out_specs=VMEM,
        compiler_params=pltpu.CompilerParams(vmem_limit_bytes=4 * MIB),
        cost_estimate=pl.CostEstimate(flops=0, bytes_accessed=MIB, transcendentals=0),
    )(both)


def first_kernel(where, mine, other, both, w, e_low, a_low, same, a, e, tiles):
    core = lax.rem(where[0], 2)
    for j in range(CHIPS):
        for t in range(3):
            tiles[t, rows_of(j, core)] = mine[j, 8 * t : 8 * t + 8]
            tiles[t, rows_of(j, 1 - core)] = other[j, 8 * t : 8 * t + 8]
    a[0:T, 0:T] = 0.5 * (tiles[0] + tiles[0].T)
    a[T:, 0:T] = tiles[1]
    a[T:, T:] = 0.5 * (tiles[2] + tiles[2].T)
    w[...] = jnp.zeros_like(w)
    e[...] = jnp.zeros_like(e)
    for i in range(2):
        o = i * B
        p = o + B
        part = leaf(a[o:p, o:p])
        w[o:p, o:p] = part
        if i:
            w[o:p, 0:o] = dot(part, e[o:p, 0:o])
        low = dot_t(a[p:, o:p], part)
        for j in range(i + 1, 4):
            r = (j - i - 1) * B
            a[j * B :, j * B : (j + 1) * B] -= dot_t(low[r:], low[r : r + B])
        e[p:, 0:p] -= dot(low, w[o:p, 0:p])
    e_low[...] = e[T:, :]
    a_low[...] = a[T:, T:]


def second_kernel(a, e_low, w, w_low):
    top = leaf(a[0:B, 0:B])
    low = dot_t(a[B:, 0:B], top)
    end = leaf(a[B:, B:] - dot_t(low, low))
    w[0:B, 0:B] = top
    w[0:B, B:] = jnp.zeros((B, B), F32)
    w[B:, 0:B] = -dot(end, dot(low, top))
    w[B:, B:] = end
    w_low[...] = dot(w[...], e_low[...])


def square(n):
    return jax.ShapeDtypeStruct((n, n), F32)


def first_factor(where, mine, other, both):
    far = pl.BlockSpec(memory_space=pl.ANY)
    return pl.pallas_call(
        first_kernel,
        out_shape=[square(T)] * 3 + [jax.ShapeDtypeStruct(both.shape, F32)],
        in_specs=[SMEM, VMEM, VMEM, far],
        out_specs=[VMEM] * 3 + [far],
        input_output_aliases={3: 3},
        scratch_shapes=[pltpu.VMEM((2 * T, 2 * T), F32), pltpu.VMEM((2 * T, T), F32), pltpu.VMEM((3, T, T), F32)],
        compiler_params=pltpu.CompilerParams(vmem_limit_bytes=12 * MIB),
        cost_estimate=pl.CostEstimate(flops=10**9, bytes_accessed=40 * MIB, transcendentals=0),
    )(where, mine, other, both)


def second_factor(a, e_low):
    return pl.pallas_call(
        second_kernel,
        out_shape=[square(T)] * 2,
        in_specs=[VMEM] * 2,
        out_specs=[VMEM] * 2,
        compiler_params=pltpu.CompilerParams(vmem_limit_bytes=12 * MIB),
        cost_estimate=pl.CostEstimate(flops=10**9, bytes_accessed=40 * MIB, transcendentals=0),
    )(a, e_low)


def split(x):
    high = x.astype(BF16)
    return high, (x - high.astype(F32)).astype(BF16)


def thirds(x):
    high = x.astype(BF16)
    rest = x - high.astype(F32)
    middle = rest.astype(BF16)
    return high, middle, (rest - middle.astype(F32)).astype(BF16)


def mul(u, v):
    return lax.dot_general(u, v, (((1,), (1,)), ((), ())), preferred_element_type=F32)


def lay(ref, at, x, order):
    parts = thirds(x)
    for i, part in enumerate(order):
        ref[:, at + i * T : at + (i + 1) * T] = parts[part]


LEFT = (0, 0, 1, 1, 0, 2)
RIGHT = (0, 1, 0, 1, 2, 0)
SIX = 6 * T
STEP = 256


def update_kernel(where, a, p, mine, other, w00, w10, w11, out, buf, panel, mirror, x_out, left, right, x_cat, y_cat, sem_a, sem_p, sem_out):
    r, c = where[0], where[1]
    core = lax.rem(r, 2)
    n_half = 4 * T * 8 // 2
    loads = [pltpu.make_async_copy(a.at[pl.ds(i * n_half, n_half)], buf.at[pl.ds(i * n_half, n_half)], sem_a.at[i]) for i in range(2)]
    fetch = pltpu.make_async_copy(p, panel, sem_p)
    fetch.start()
    for load in loads:
        load.start()
    for i, t in enumerate((w00, w10, w11)):
        lay(right, i * SIX, t[...], RIGHT)

    def solve(first, second, stride, start, cat, order, keep):
        lay(left, 0, first, LEFT)
        lay(left, SIX, second, LEFT)
        for i in range(0, 4 * T, STEP):
            rows = slice(i, i + STEP)
            x0 = mul(left[rows, 0:SIX], right[:, 0:SIX])
            x1 = mul(left[rows], right[:, SIX:])
            if keep:
                x_out[rows] = jnp.where(c == 0, x0, x1)
            tile = (lax.broadcasted_iota(jnp.int32, (STEP, 1), 0) + i) // T * stride + start
            for k, x in enumerate((x0, x1)):
                parts = split(jnp.where(tile > k, x, 0.0))
                for j, part in enumerate(order):
                    at = (2 * j + k) * T
                    cat[rows, at : at + T] = parts[part]

    for j in range(CHIPS):
        for k in range(2):
            for n in range(4):
                at = LEAD + 32 * k + 8 * n
                mirror[k, n, rows_of(j, core)] = mine[j, at : at + 8]
                mirror[k, n, rows_of(j, 1 - core)] = other[j, at : at + 8]
    solve(mirror[0].reshape(4 * T, T), mirror[1].reshape(4 * T, T), 8, c, y_cat, (0, 0, 1), False)
    fetch.wait()
    first = jnp.concatenate([panel[0], panel[7], panel[6], panel[5]], axis=0)
    solve(first, panel[1:5].reshape(4 * T, T), 32, r, x_cat, (0, 1, 0), True)

    rows = 2 * T
    stores = []
    for i in range(2):
        loads[i].wait()
        span = slice(i * rows, (i + 1) * rows)
        for n in range(4):
            cols = slice(n * T, (n + 1) * T)
            product = mul(x_cat[span], y_cat[cols])
            for half in range(2):
                at = pl.ds(i * n_half + half * 4 + n, rows, stride=8)
                buf[at, :] = buf[at, :] - product[:, half * B : (half + 1) * B]

        @pl.when(c < 2)
        def _():
            row = lax.broadcasted_iota(jnp.int32, (rows, T), 0) + i * rows
            col = lax.broadcasted_iota(jnp.int32, (rows, T), 1)
            tile = row // T * 32 + r
            keep = (tile > c) | ((tile == c) & (lax.rem(row, T) >= col))
            x = jnp.where(keep, x_out[span], 0.0)
            for half in range(2):
                buf[pl.ds(i * n_half + half * 4, rows, stride=8), :] = x[:, half * B : (half + 1) * B]

        at = pl.ds(i * n_half, n_half)
        stores.append(pltpu.make_async_copy(buf.at[at], out.at[at], sem_out.at[i]))
        stores[i].start()
    for store in stores:
        store.wait()


def update(where, a, panel, mine, other, w):
    hbm = pl.BlockSpec(memory_space=pltpu.HBM)
    a, panel = (pltpu.with_memory_space_constraint(t, pltpu.HBM) for t in (a, panel))
    return pl.pallas_call(
        update_kernel,
        out_shape=jax.ShapeDtypeStruct(a.shape, F32),
        in_specs=[SMEM, hbm, hbm] + [VMEM] * 5,
        out_specs=hbm,
        scratch_shapes=[
            pltpu.VMEM((4 * T * 8, B), F32),
            pltpu.VMEM((8, T, T), F32),
            pltpu.VMEM((2, 4, T, T), F32),
            pltpu.VMEM((4 * T, T), F32),
            pltpu.VMEM((4 * T, 2 * SIX), BF16),
            pltpu.VMEM((T, 3 * SIX), BF16),
            pltpu.VMEM((4 * T, SIX), BF16),
            pltpu.VMEM((4 * T, SIX), BF16),
            pltpu.SemaphoreType.DMA((2,)),
            pltpu.SemaphoreType.DMA,
            pltpu.SemaphoreType.DMA((2,)),
        ],
        compiler_params=pltpu.CompilerParams(vmem_limit_bytes=38 * MIB),
        cost_estimate=pl.CostEstimate(flops=8 * 10**9, bytes_accessed=12 * MIB, transcendentals=0),
    )(where, a, panel, mine, other, *w)


def per_device(matrix):
    r = lax.axis_index("row")
    c = lax.axis_index("col")
    where = jnp.stack([r, c]).astype(jnp.int32)
    flat = matrix.reshape(4, T, 4, 2, B).transpose(0, 1, 3, 2, 4).reshape(4 * T * 8, B)
    column = matrix[:, :, 0, :]
    first = column[0]

    got = [lax.ppermute(column[m], "col", [(0, 8 - m), (1, 1 + m)]) for m in (1, 2, 3)]
    pieces = lax.all_to_all(first.reshape(32, 8, T), "row", 0, 0)
    spread, tile = outward(where, pieces, first, got)
    both, share = inward(lax.all_to_all(spread, "col", 0, 0), tile)
    panel = lax.all_gather(share, "col", axis=0)

    cores = [[2 * j + k for j in range(CHIPS)] for k in range(2)]
    swap = [(i, i ^ 1) for i in range(32)]
    both = lax.all_to_all(both, "row", 0, 0, axis_index_groups=cores)
    lead = head(both)
    w00, e_low, a_low, both = first_factor(where, lead, lax.ppermute(lead, "row", swap), both)
    w11, w10 = second_factor(a_low, e_low)
    out = update(where, flat, panel, both, lax.ppermute(both, "row", swap), (w00, w10, w11))
    return out.reshape(4, T, 2, 4, B).transpose(0, 1, 3, 2, 4).reshape(4, T, 4, T)


def solution(mesh):
    spec = P(None, "row", None, "col")
    return jax.shard_map(per_device, mesh=mesh, in_specs=(spec,), out_specs=spec, check_vma=False)
```

```python
import jax
import jax.numpy as jnp
from jax import lax
from jax.experimental import pallas as pl
from jax.experimental.pallas import tpu as pltpu
from jax.sharding import PartitionSpec as P

HI = lax.Precision.HIGHEST
F32 = jnp.float32
BF16 = jnp.bfloat16
B = 128
T = 256
MIB = 1024 * 1024


def dot(a, b):
    return lax.dot_general(a, b, (((1,), (0,)), ((), ())), precision=HI, preferred_element_type=F32)


def dot_t(a, b):
    return lax.dot_general(a, b, (((1,), (1,)), ((), ())), precision=HI, preferred_element_type=F32)


def leaf(d):
    n = d.shape[0]
    sub = lax.broadcasted_iota(jnp.int32, (8, B), 0)
    row = lax.broadcasted_iota(jnp.int32, (n, B), 0)
    col = lax.broadcasted_iota(jnp.int32, (n, B), 1)
    e = jnp.where(row == col, 1.0, 0.0).astype(F32)
    out = []
    for q in range(n // 8):
        left = n - 8 * q
        rest = left - 8
        cols = [jnp.broadcast_to(d[:, 8 * q + k : 8 * q + k + 1], (left, B)) for k in range(8)]
        tops, lows = [], []
        scale = jnp.zeros((8, B), F32)
        for k in range(8):
            pivot = jnp.broadcast_to(cols[k][k : k + 1, :], (8, B))
            reciprocal = 1.0 / pivot
            scale = jnp.where(sub == k, lax.rsqrt(pivot), scale)
            top = jnp.where(sub > k, cols[k][:8] * reciprocal, 0.0)
            tops.append(top)
            if rest:
                low = cols[k][8:] * jnp.broadcast_to(reciprocal[:1], (rest, B))
                lows.append(low)
            for l in range(k + 1, 8):
                u = cols[l][k : k + 1, :]
                t = cols[l][:8] - top * jnp.broadcast_to(u, (8, B))
                if rest:
                    r = cols[l][8:] - low * jnp.broadcast_to(u, (rest, B))
                    t = jnp.concatenate([t, r], 0)
                cols[l] = t
        d_top, e_top = d[:8], e[:8]
        d_rows, e_rows = [], []
        for k in range(8):
            a, b = d_top[k : k + 1, :], e_top[k : k + 1, :]
            d_rows.append(a)
            e_rows.append(b)
            d_top = d_top - tops[k] * jnp.broadcast_to(a, (8, B))
            e_top = e_top - tops[k] * jnp.broadcast_to(b, (8, B))
        out.append(e_top * scale)
        if rest:
            d, e = d[8:], e[8:]
            for k in range(8):
                d = d - lows[k] * jnp.broadcast_to(d_rows[k], (rest, B))
                e = e - lows[k] * jnp.broadcast_to(e_rows[k], (rest, B))
    return jnp.concatenate(out, 0)


VMEM = pl.BlockSpec(memory_space=pltpu.VMEM)
ANY = pl.BlockSpec(memory_space=pl.ANY)
SMEM = pl.BlockSpec(memory_space=pltpu.SMEM)
CHIPS = 16
LEAD = 24


def rows_of(chip, core):
    return pl.ds(pl.multiple_of(16 * chip + 8 * core, 8), 8)


def small(kernel, outs, specs, *args):
    return pl.pallas_call(
        kernel,
        out_shape=[jax.ShapeDtypeStruct(shape, F32) for shape in outs],
        in_specs=specs,
        out_specs=[VMEM] * len(outs),
        compiler_params=pltpu.CompilerParams(vmem_limit_bytes=4 * MIB),
        cost_estimate=pl.CostEstimate(flops=0, bytes_accessed=2 * MIB, transcendentals=0),
    )(*args)


def outward_kernel(where, pieces, first, got1, got2, got3, out, share):
    for z in range(8):
        for i, tile in enumerate((z, z + 8, z + 16, z + 24, 0, 1)):
            out[z, 8 * i : 8 * i + 8] = pieces[tile]
    share[...] = jnp.where(where[1] < 2, first[...], got1[...] + got2[...] + got3[...])


def inward_kernel(lines, tile, out, share):
    for j in range(CHIPS):
        out[j, 0:16] = lines[0, 32:48]
        out[j, 16:LEAD] = lines[1, 40:48]
        out[j, LEAD : LEAD + 32] = lines[0, 0:32]
        out[j, LEAD + 32 :] = lines[1, 0:32]
    share[...] = tile[...]


def head_kernel(both, right, left, ready1, ready2, lead, up, down, top, bottom):
    lead[...] = both[:, 0:LEAD]
    up[...] = right[...]
    down[...] = left[...]
    top[...] = right[0:B]
    bottom[...] = left[B:]


def first_kernel(where, mine, other, both, w, e_low, a_low, same, a, e, tiles):
    core = lax.rem(where[0], 2)
    for j in range(CHIPS):
        for t in range(3):
            tiles[t, rows_of(j, core)] = mine[j, 8 * t : 8 * t + 8]
            tiles[t, rows_of(j, 1 - core)] = other[j, 8 * t : 8 * t + 8]
    a[0:T, 0:T] = 0.5 * (tiles[0] + tiles[0].T)
    a[T:, 0:T] = tiles[1]
    a[T:, T:] = 0.5 * (tiles[2] + tiles[2].T)
    w[...] = jnp.zeros_like(w)
    e[...] = jnp.zeros_like(e)
    for i in range(2):
        o = i * B
        p = o + B
        part = leaf(a[o:p, o:p])
        w[o:p, o:p] = part
        if i:
            w[o:p, 0:o] = dot(part, e[o:p, 0:o])
        low = dot_t(a[p:, o:p], part)
        for j in range(i + 1, 4):
            r = (j - i - 1) * B
            a[j * B :, j * B : (j + 1) * B] -= dot_t(low[r:], low[r : r + B])
        e[p:, 0:p] -= dot(low, w[o:p, 0:p])
    e_low[...] = e[T:, :]
    a_low[...] = a[T:, T:]


def second_kernel(a, e_low, w, w_low):
    top = leaf(a[0:B, 0:B])
    low = dot_t(a[B:, 0:B], top)
    end = leaf(a[B:, B:] - dot_t(low, low))
    w[0:B, 0:B] = top
    w[0:B, B:] = jnp.zeros((B, B), F32)
    w[B:, 0:B] = -dot(end, dot(low, top))
    w[B:, B:] = end
    w_low[...] = dot(w[...], e_low[...])


def square(n):
    return jax.ShapeDtypeStruct((n, n), F32)


def first_factor(where, mine, other, both):
    far = pl.BlockSpec(memory_space=pl.ANY)
    return pl.pallas_call(
        first_kernel,
        out_shape=[square(T)] * 3 + [jax.ShapeDtypeStruct(both.shape, F32)],
        in_specs=[SMEM, VMEM, VMEM, far],
        out_specs=[VMEM] * 3 + [far],
        input_output_aliases={3: 3},
        scratch_shapes=[pltpu.VMEM((2 * T, 2 * T), F32), pltpu.VMEM((2 * T, T), F32), pltpu.VMEM((3, T, T), F32)],
        compiler_params=pltpu.CompilerParams(vmem_limit_bytes=12 * MIB),
        cost_estimate=pl.CostEstimate(flops=10**9, bytes_accessed=40 * MIB, transcendentals=0),
    )(where, mine, other, both)


def second_factor(a, e_low):
    return pl.pallas_call(
        second_kernel,
        out_shape=[square(T)] * 2,
        in_specs=[VMEM] * 2,
        out_specs=[VMEM] * 2,
        compiler_params=pltpu.CompilerParams(vmem_limit_bytes=12 * MIB),
        cost_estimate=pl.CostEstimate(flops=10**9, bytes_accessed=40 * MIB, transcendentals=0),
    )(a, e_low)


def split(x):
    high = x.astype(BF16)
    return high, (x - high.astype(F32)).astype(BF16)


def thirds(x):
    high = x.astype(BF16)
    rest = x - high.astype(F32)
    middle = rest.astype(BF16)
    return high, middle, (rest - middle.astype(F32)).astype(BF16)


def mul(u, v):
    return lax.dot_general(u, v, (((1,), (1,)), ((), ())), preferred_element_type=F32)


def lay(ref, at, x, order):
    parts = thirds(x)
    for i, part in enumerate(order):
        ref[:, at + i * T : at + (i + 1) * T] = parts[part]


LEFT = (0, 0, 1, 1, 0, 2)
RIGHT = (0, 1, 0, 1, 2, 0)
SIX = 6 * T
STEP = 256


def update_kernel(where, a, *refs):
    panels, refs = refs[:9], refs[9:]
    mine, other, w00, w10, w11, out, buf, panel, mirror, x_out, left, right, x_cat, y_cat, sem_a, sem_out = refs
    r, c = where[0], where[1]
    core = lax.rem(r, 2)
    n_half = 4 * T * 8 // 2
    loads = [pltpu.make_async_copy(a.at[pl.ds(i * n_half, n_half)], buf.at[pl.ds(i * n_half, n_half)], sem_a.at[i]) for i in range(2)]
    for load in loads:
        load.start()
    for i, t in enumerate((w00, w10, w11)):
        lay(right, i * SIX, t[...], RIGHT)

    def solve(first, second, stride, start, cat, order, keep):
        lay(left, 0, first, LEFT)
        lay(left, SIX, second, LEFT)
        for i in range(0, 4 * T, STEP):
            rows = slice(i, i + STEP)
            x0 = mul(left[rows, 0:SIX], right[:, 0:SIX])
            x1 = mul(left[rows], right[:, SIX:])
            if keep:
                x_out[rows] = jnp.where(c == 0, x0, x1)
            tile = (lax.broadcasted_iota(jnp.int32, (STEP, 1), 0) + i) // T * stride + start
            for k, x in enumerate((x0, x1)):
                parts = split(jnp.where(tile > k, x, 0.0))
                for j, part in enumerate(order):
                    at = (2 * j + k) * T
                    cat[rows, at : at + T] = parts[part]

    for j in range(CHIPS):
        for k in range(2):
            for n in range(4):
                at = LEAD + 32 * k + 8 * n
                mirror[k, n, rows_of(j, core)] = mine[j, at : at + 8]
                mirror[k, n, rows_of(j, 1 - core)] = other[j, at : at + 8]
    solve(mirror[0].reshape(4 * T, T), mirror[1].reshape(4 * T, T), 8, c, y_cat, (0, 0, 1), False)
    for j, part in zip((0, 1, 2, 3, 5, 6, 7), panels):
        panel[lax.rem(c - j + 8, 8)] = part[...]
    panel[lax.rem(c + 4, 8), 0:B] = panels[7][...]
    panel[lax.rem(c + 4, 8), B:] = panels[8][...]
    first = jnp.concatenate([panel[0], panel[7], panel[6], panel[5]], axis=0)
    solve(first, panel[1:5].reshape(4 * T, T), 32, r, x_cat, (0, 1, 0), True)

    rows = 2 * T
    stores = []
    for i in range(2):
        loads[i].wait()
        span = slice(i * rows, (i + 1) * rows)
        for n in range(4):
            cols = slice(n * T, (n + 1) * T)
            product = mul(x_cat[span], y_cat[cols])
            for half in range(2):
                at = pl.ds(i * n_half + half * 4 + n, rows, stride=8)
                buf[at, :] = buf[at, :] - product[:, half * B : (half + 1) * B]

        @pl.when(c < 2)
        def _():
            row = lax.broadcasted_iota(jnp.int32, (rows, T), 0) + i * rows
            col = lax.broadcasted_iota(jnp.int32, (rows, T), 1)
            tile = row // T * 32 + r
            keep = (tile > c) | ((tile == c) & (lax.rem(row, T) >= col))
            x = jnp.where(keep, x_out[span], 0.0)
            for half in range(2):
                buf[pl.ds(i * n_half + half * 4, rows, stride=8), :] = x[:, half * B : (half + 1) * B]

        at = pl.ds(i * n_half, n_half)
        stores.append(pltpu.make_async_copy(buf.at[at], out.at[at], sem_out.at[i]))
        stores[i].start()
    for store in stores:
        store.wait()


def update(where, a, panels, mine, other, w):
    hbm = pl.BlockSpec(memory_space=pltpu.HBM)
    a = pltpu.with_memory_space_constraint(a, pltpu.HBM)
    return pl.pallas_call(
        update_kernel,
        out_shape=jax.ShapeDtypeStruct(a.shape, F32),
        in_specs=[SMEM, hbm] + [VMEM] * 14,
        out_specs=hbm,
        scratch_shapes=[
            pltpu.VMEM((4 * T * 8, B), F32),
            pltpu.VMEM((8, T, T), F32),
            pltpu.VMEM((2, 4, T, T), F32),
            pltpu.VMEM((4 * T, T), F32),
            pltpu.VMEM((4 * T, 2 * SIX), BF16),
            pltpu.VMEM((T, 3 * SIX), BF16),
            pltpu.VMEM((4 * T, SIX), BF16),
            pltpu.VMEM((4 * T, SIX), BF16),
            pltpu.SemaphoreType.DMA((2,)),
            pltpu.SemaphoreType.DMA((2,)),
        ],
        compiler_params=pltpu.CompilerParams(vmem_limit_bytes=38 * MIB),
        cost_estimate=pl.CostEstimate(flops=8 * 10**9, bytes_accessed=12 * MIB, transcendentals=0),
    )(where, a, *panels, mine, other, *w)


def along(x, step):
    return lax.ppermute(x, "col", [(z, (z + step) % 8) for z in range(8)])


def per_device(matrix):
    r = lax.axis_index("row")
    c = lax.axis_index("col")
    where = jnp.stack([r, c]).astype(jnp.int32)
    flat = matrix.reshape(4, T, 4, 2, B).transpose(0, 1, 3, 2, 4).reshape(4 * T * 8, B)
    column = matrix[:, :, 0, :]
    first = column[0]
    tile = (T, T)
    half = (B, T)

    got = [lax.ppermute(column[m], "col", [(0, 8 - m), (1, 1 + m)]) for m in (1, 2, 3)]
    pieces = lax.all_to_all(first.reshape(32, 8, T), "row", 0, 0)
    spread, share = small(outward_kernel, [(8, 48, T), tile], [SMEM] + [VMEM] * 5, where, pieces, first, *got)
    lines = lax.all_to_all(spread, "col", 0, 0)
    both, share = small(inward_kernel, [(CHIPS, LEAD + 64, T), tile], [VMEM] * 2, lines, share)
    near = [along(share, step) for step in (1, 2, -2, -1)]

    cores = [[2 * j + k for j in range(CHIPS)] for k in range(2)]
    swap = [(i, i ^ 1) for i in range(32)]
    both = lax.all_to_all(both, "row", 0, 0, axis_index_groups=cores)
    lead, up, down, top, bottom = small(
        head_kernel, [(CHIPS, LEAD, T), tile, tile, half, half], [VMEM] * 3 + [ANY] * 2, both, near[1], near[2], near[0], near[3]
    )
    far = [along(up, 1), along(down, -1), along(top, 2), along(bottom, -2)]
    w00, e_low, a_low, both = first_factor(where, lead, lax.ppermute(lead, "row", swap), both)
    w11, w10 = second_factor(a_low, e_low)
    panels = [share, near[0], near[1], far[0], far[1], near[2], near[3], far[2], far[3]]
    out = update(where, flat, panels, both, lax.ppermute(both, "row", swap), (w00, w10, w11))
    return out.reshape(4, T, 2, 4, B).transpose(0, 1, 3, 2, 4).reshape(4, T, 4, T)


def solution(mesh):
    spec = P(None, "row", None, "col")
    return jax.shard_map(per_device, mesh=mesh, in_specs=(spec,), out_specs=spec, check_vma=False)
```

```python
import jax
import jax.numpy as jnp
from jax import lax
from jax.experimental import pallas as pl
from jax.experimental.pallas import tpu as pltpu
from jax.sharding import PartitionSpec as P

HI = lax.Precision.HIGHEST
F32 = jnp.float32
BF16 = jnp.bfloat16
B = 128
T = 256
MIB = 1024 * 1024


def dot(a, b):
    return lax.dot_general(a, b, (((1,), (0,)), ((), ())), precision=HI, preferred_element_type=F32)


def dot_t(a, b):
    return lax.dot_general(a, b, (((1,), (1,)), ((), ())), precision=HI, preferred_element_type=F32)


def leaf(d):
    n = d.shape[0]
    sub = lax.broadcasted_iota(jnp.int32, (8, B), 0)
    row = lax.broadcasted_iota(jnp.int32, (n, B), 0)
    col = lax.broadcasted_iota(jnp.int32, (n, B), 1)
    e = jnp.where(row == col, 1.0, 0.0).astype(F32)
    out = []
    for q in range(n // 8):
        left = n - 8 * q
        rest = left - 8
        cols = [jnp.broadcast_to(d[:, 8 * q + k : 8 * q + k + 1], (left, B)) for k in range(8)]
        tops, lows = [], []
        scale = jnp.zeros((8, B), F32)
        for k in range(8):
            pivot = jnp.broadcast_to(cols[k][k : k + 1, :], (8, B))
            reciprocal = 1.0 / pivot
            scale = jnp.where(sub == k, lax.rsqrt(pivot), scale)
            top = jnp.where(sub > k, cols[k][:8] * reciprocal, 0.0)
            tops.append(top)
            if rest:
                low = cols[k][8:] * jnp.broadcast_to(reciprocal[:1], (rest, B))
                lows.append(low)
            for l in range(k + 1, 8):
                u = cols[l][k : k + 1, :]
                t = cols[l][:8] - top * jnp.broadcast_to(u, (8, B))
                if rest:
                    r = cols[l][8:] - low * jnp.broadcast_to(u, (rest, B))
                    t = jnp.concatenate([t, r], 0)
                cols[l] = t
        d_top, e_top = d[:8], e[:8]
        d_rows, e_rows = [], []
        for k in range(8):
            a, b = d_top[k : k + 1, :], e_top[k : k + 1, :]
            d_rows.append(a)
            e_rows.append(b)
            d_top = d_top - tops[k] * jnp.broadcast_to(a, (8, B))
            e_top = e_top - tops[k] * jnp.broadcast_to(b, (8, B))
        out.append(e_top * scale)
        if rest:
            d, e = d[8:], e[8:]
            for k in range(8):
                d = d - lows[k] * jnp.broadcast_to(d_rows[k], (rest, B))
                e = e - lows[k] * jnp.broadcast_to(e_rows[k], (rest, B))
    return jnp.concatenate(out, 0)


VMEM = pl.BlockSpec(memory_space=pltpu.VMEM)
ANY = pl.BlockSpec(memory_space=pl.ANY)
SMEM = pl.BlockSpec(memory_space=pltpu.SMEM)
CHIPS = 16
LEAD = 24


def rows_of(chip, core):
    return pl.ds(pl.multiple_of(16 * chip + 8 * core, 8), 8)


def small(kernel, outs, specs, *args):
    return pl.pallas_call(
        kernel,
        out_shape=[jax.ShapeDtypeStruct(shape, F32) for shape in outs],
        in_specs=specs,
        out_specs=[VMEM] * len(outs),
        compiler_params=pltpu.CompilerParams(vmem_limit_bytes=4 * MIB),
        cost_estimate=pl.CostEstimate(flops=0, bytes_accessed=2 * MIB, transcendentals=0),
    )(*args)


def column_kernel(a, *refs):
    outs, (buf, sem) = refs[:4], refs[4:]
    size = 8 * T
    loads = [pltpu.make_async_copy(a.at[pl.ds(m * size, size)], buf.at[pl.ds(m * size, size)], sem.at[m]) for m in range(4)]
    for load in loads:
        load.start()
    for m in range(4):
        loads[m].wait()
        for half in range(2):
            outs[m][:, half * B : (half + 1) * B] = buf[pl.ds(m * size + half * 4, T, stride=8), :]


def tile_column(a):
    return pl.pallas_call(
        column_kernel,
        out_shape=[square(T)] * 4,
        in_specs=[pl.BlockSpec(memory_space=pltpu.HBM)],
        out_specs=[VMEM] * 4,
        scratch_shapes=[pltpu.VMEM((4 * T * 8, B), F32), pltpu.SemaphoreType.DMA((4,))],
        compiler_params=pltpu.CompilerParams(vmem_limit_bytes=8 * MIB),
        cost_estimate=pl.CostEstimate(flops=0, bytes_accessed=5 * MIB, transcendentals=0),
    )(pltpu.with_memory_space_constraint(a, pltpu.HBM))


def outward_kernel(where, pieces, first, got1, got2, got3, out, share):
    for z in range(8):
        for i, tile in enumerate((z, z + 8, z + 16, z + 24, 0, 1)):
            out[z, 8 * i : 8 * i + 8] = pieces[tile]
    share[...] = jnp.where(where[1] < 2, first[...], got1[...] + got2[...] + got3[...])


def inward_kernel(lines, tile, out, share):
    for j in range(CHIPS):
        out[j, 0:16] = lines[0, 32:48]
        out[j, 16:LEAD] = lines[1, 40:48]
        out[j, LEAD : LEAD + 32] = lines[0, 0:32]
        out[j, LEAD + 32 :] = lines[1, 0:32]
    share[...] = tile[...]


def head_kernel(both, right, left, ready1, ready2, lead, up, down, top, bottom):
    lead[...] = both[:, 0:LEAD]
    up[...] = right[...]
    down[...] = left[...]
    top[...] = right[0:B]
    bottom[...] = left[B:]


def first_kernel(where, mine, other, both, w, e_low, a_low, same, a, e, tiles):
    core = lax.rem(where[0], 2)
    for j in range(CHIPS):
        for t in range(3):
            tiles[t, rows_of(j, core)] = mine[j, 8 * t : 8 * t + 8]
            tiles[t, rows_of(j, 1 - core)] = other[j, 8 * t : 8 * t + 8]
    a[0:T, 0:T] = 0.5 * (tiles[0] + tiles[0].T)
    a[T:, 0:T] = tiles[1]
    a[T:, T:] = 0.5 * (tiles[2] + tiles[2].T)
    w[...] = jnp.zeros_like(w)
    e[...] = jnp.zeros_like(e)
    for i in range(2):
        o = i * B
        p = o + B
        part = leaf(a[o:p, o:p])
        w[o:p, o:p] = part
        if i:
            w[o:p, 0:o] = dot(part, e[o:p, 0:o])
        low = dot_t(a[p:, o:p], part)
        for j in range(i + 1, 4):
            r = (j - i - 1) * B
            a[j * B :, j * B : (j + 1) * B] -= dot_t(low[r:], low[r : r + B])
        e[p:, 0:p] -= dot(low, w[o:p, 0:p])
    e_low[...] = e[T:, :]
    a_low[...] = a[T:, T:]


def second_kernel(a, e_low, w, w_low):
    top = leaf(a[0:B, 0:B])
    low = dot_t(a[B:, 0:B], top)
    end = leaf(a[B:, B:] - dot_t(low, low))
    w[0:B, 0:B] = top
    w[0:B, B:] = jnp.zeros((B, B), F32)
    w[B:, 0:B] = -dot(end, dot(low, top))
    w[B:, B:] = end
    w_low[...] = dot(w[...], e_low[...])


def square(n):
    return jax.ShapeDtypeStruct((n, n), F32)


def first_factor(where, mine, other, both):
    far = pl.BlockSpec(memory_space=pl.ANY)
    return pl.pallas_call(
        first_kernel,
        out_shape=[square(T)] * 3 + [jax.ShapeDtypeStruct(both.shape, F32)],
        in_specs=[SMEM, VMEM, VMEM, far],
        out_specs=[VMEM] * 3 + [far],
        input_output_aliases={3: 3},
        scratch_shapes=[pltpu.VMEM((2 * T, 2 * T), F32), pltpu.VMEM((2 * T, T), F32), pltpu.VMEM((3, T, T), F32)],
        compiler_params=pltpu.CompilerParams(vmem_limit_bytes=12 * MIB),
        cost_estimate=pl.CostEstimate(flops=10**9, bytes_accessed=40 * MIB, transcendentals=0),
    )(where, mine, other, both)


def second_factor(a, e_low):
    return pl.pallas_call(
        second_kernel,
        out_shape=[square(T)] * 2,
        in_specs=[VMEM] * 2,
        out_specs=[VMEM] * 2,
        compiler_params=pltpu.CompilerParams(vmem_limit_bytes=12 * MIB),
        cost_estimate=pl.CostEstimate(flops=10**9, bytes_accessed=40 * MIB, transcendentals=0),
    )(a, e_low)


def split(x):
    high = x.astype(BF16)
    return high, (x - high.astype(F32)).astype(BF16)


def thirds(x):
    high = x.astype(BF16)
    rest = x - high.astype(F32)
    middle = rest.astype(BF16)
    return high, middle, (rest - middle.astype(F32)).astype(BF16)


def mul(u, v):
    return lax.dot_general(u, v, (((1,), (1,)), ((), ())), preferred_element_type=F32)


def lay(ref, at, x, order):
    parts = thirds(x)
    for i, part in enumerate(order):
        ref[:, at + i * T : at + (i + 1) * T] = parts[part]


LEFT = (0, 0, 1, 1, 0, 2)
RIGHT = (0, 1, 0, 1, 2, 0)
SIX = 6 * T
STEP = 256


def update_kernel(where, a, *refs):
    panels, refs = refs[:9], refs[9:]
    mine, other, w00, w10, w11, out, buf, panel, mirror, x_out, left, right, x_cat, y_cat, sem_a, sem_out = refs
    r, c = where[0], where[1]
    core = lax.rem(r, 2)
    n_half = 4 * T * 8 // 2
    loads = [pltpu.make_async_copy(a.at[pl.ds(i * n_half, n_half)], buf.at[pl.ds(i * n_half, n_half)], sem_a.at[i]) for i in range(2)]
    for load in loads:
        load.start()
    for i, t in enumerate((w00, w10, w11)):
        lay(right, i * SIX, t[...], RIGHT)

    def solve(first, second, stride, start, cat, order, keep):
        lay(left, 0, first, LEFT)
        lay(left, SIX, second, LEFT)
        for i in range(0, 4 * T, STEP):
            rows = slice(i, i + STEP)
            x0 = mul(left[rows, 0:SIX], right[:, 0:SIX])
            x1 = mul(left[rows], right[:, SIX:])
            if keep:
                x_out[rows] = jnp.where(c == 0, x0, x1)
            tile = (lax.broadcasted_iota(jnp.int32, (STEP, 1), 0) + i) // T * stride + start
            for k, x in enumerate((x0, x1)):
                parts = split(jnp.where(tile > k, x, 0.0))
                for j, part in enumerate(order):
                    at = (2 * j + k) * T
                    cat[rows, at : at + T] = parts[part]

    for j in range(CHIPS):
        for k in range(2):
            for n in range(4):
                at = LEAD + 32 * k + 8 * n
                mirror[k, n, rows_of(j, core)] = mine[j, at : at + 8]
                mirror[k, n, rows_of(j, 1 - core)] = other[j, at : at + 8]
    solve(mirror[0].reshape(4 * T, T), mirror[1].reshape(4 * T, T), 8, c, y_cat, (0, 0, 1), False)
    for j, part in zip((0, 1, 2, 3, 5, 6, 7), panels):
        panel[lax.rem(c - j + 8, 8)] = part[...]
    panel[lax.rem(c + 4, 8), 0:B] = panels[7][...]
    panel[lax.rem(c + 4, 8), B:] = panels[8][...]
    first = jnp.concatenate([panel[0], panel[7], panel[6], panel[5]], axis=0)
    solve(first, panel[1:5].reshape(4 * T, T), 32, r, x_cat, (0, 1, 0), True)

    rows = 2 * T
    stores = []
    for i in range(2):
        loads[i].wait()
        span = slice(i * rows, (i + 1) * rows)
        for n in range(4):
            cols = slice(n * T, (n + 1) * T)
            product = mul(x_cat[span], y_cat[cols])
            for half in range(2):
                at = pl.ds(i * n_half + half * 4 + n, rows, stride=8)
                buf[at, :] = buf[at, :] - product[:, half * B : (half + 1) * B]

        @pl.when(c < 2)
        def _():
            row = lax.broadcasted_iota(jnp.int32, (rows, T), 0) + i * rows
            col = lax.broadcasted_iota(jnp.int32, (rows, T), 1)
            tile = row // T * 32 + r
            keep = (tile > c) | ((tile == c) & (lax.rem(row, T) >= col))
            x = jnp.where(keep, x_out[span], 0.0)
            for half in range(2):
                buf[pl.ds(i * n_half + half * 4, rows, stride=8), :] = x[:, half * B : (half + 1) * B]

        at = pl.ds(i * n_half, n_half)
        stores.append(pltpu.make_async_copy(buf.at[at], out.at[at], sem_out.at[i]))
        stores[i].start()
    for store in stores:
        store.wait()


def update(where, a, panels, mine, other, w):
    hbm = pl.BlockSpec(memory_space=pltpu.HBM)
    a = pltpu.with_memory_space_constraint(a, pltpu.HBM)
    return pl.pallas_call(
        update_kernel,
        out_shape=jax.ShapeDtypeStruct(a.shape, F32),
        in_specs=[SMEM, hbm] + [VMEM] * 14,
        out_specs=hbm,
        scratch_shapes=[
            pltpu.VMEM((4 * T * 8, B), F32),
            pltpu.VMEM((8, T, T), F32),
            pltpu.VMEM((2, 4, T, T), F32),
            pltpu.VMEM((4 * T, T), F32),
            pltpu.VMEM((4 * T, 2 * SIX), BF16),
            pltpu.VMEM((T, 3 * SIX), BF16),
            pltpu.VMEM((4 * T, SIX), BF16),
            pltpu.VMEM((4 * T, SIX), BF16),
            pltpu.SemaphoreType.DMA((2,)),
            pltpu.SemaphoreType.DMA((2,)),
        ],
        compiler_params=pltpu.CompilerParams(vmem_limit_bytes=38 * MIB),
        cost_estimate=pl.CostEstimate(flops=8 * 10**9, bytes_accessed=12 * MIB, transcendentals=0),
    )(where, a, *panels, mine, other, *w)


def along(x, step):
    return lax.ppermute(x, "col", [(z, (z + step) % 8) for z in range(8)])


def per_device(matrix):
    r = lax.axis_index("row")
    c = lax.axis_index("col")
    where = jnp.stack([r, c]).astype(jnp.int32)
    flat = matrix.reshape(4, T, 4, 2, B).transpose(0, 1, 3, 2, 4).reshape(4 * T * 8, B)
    column = tile_column(flat)
    first = column[0]
    tile = (T, T)
    half = (B, T)

    got = [lax.ppermute(column[m], "col", [(0, 8 - m), (1, 1 + m)]) for m in (1, 2, 3)]
    pieces = lax.all_to_all(first.reshape(32, 8, T), "row", 0, 0)
    spread, share = small(outward_kernel, [(8, 48, T), tile], [SMEM] + [VMEM] * 5, where, pieces, first, *got)
    lines = lax.all_to_all(spread, "col", 0, 0)
    both, share = small(inward_kernel, [(CHIPS, LEAD + 64, T), tile], [VMEM] * 2, lines, share)
    near = [along(share, step) for step in (1, 2, -2, -1)]

    cores = [[2 * j + k for j in range(CHIPS)] for k in range(2)]
    swap = [(i, i ^ 1) for i in range(32)]
    both = lax.all_to_all(both, "row", 0, 0, axis_index_groups=cores)
    lead, up, down, top, bottom = small(
        head_kernel, [(CHIPS, LEAD, T), tile, tile, half, half], [VMEM] * 3 + [ANY] * 2, both, near[1], near[2], near[0], near[3]
    )
    far = [along(up, 1), along(down, -1), along(top, 2), along(bottom, -2)]
    w00, e_low, a_low, both = first_factor(where, lead, lax.ppermute(lead, "row", swap), both)
    w11, w10 = second_factor(a_low, e_low)
    panels = [share, near[0], near[1], far[0], far[1], near[2], near[3], far[2], far[3]]
    out = update(where, flat, panels, both, lax.ppermute(both, "row", swap), (w00, w10, w11))
    return out.reshape(4, T, 2, 4, B).transpose(0, 1, 3, 2, 4).reshape(4, T, 4, T)


def solution(mesh):
    spec = P(None, "row", None, "col")
    return jax.shard_map(per_device, mesh=mesh, in_specs=(spec,), out_specs=spec, check_vma=False)
```

```python
import jax
import jax.numpy as jnp
from jax import lax
from jax.experimental import pallas as pl
from jax.experimental.pallas import tpu as pltpu
from jax.sharding import PartitionSpec as P

HI = lax.Precision.HIGHEST
F32 = jnp.float32
BF16 = jnp.bfloat16
B = 128
T = 256
MIB = 1024 * 1024


def dot(a, b):
    return lax.dot_general(a, b, (((1,), (0,)), ((), ())), precision=HI, preferred_element_type=F32)


def dot_t(a, b):
    return lax.dot_general(a, b, (((1,), (1,)), ((), ())), precision=HI, preferred_element_type=F32)


def leaf(d):
    n = d.shape[0]
    sub = lax.broadcasted_iota(jnp.int32, (8, B), 0)
    row = lax.broadcasted_iota(jnp.int32, (n, B), 0)
    col = lax.broadcasted_iota(jnp.int32, (n, B), 1)
    e = jnp.where(row == col, 1.0, 0.0).astype(F32)
    out = []
    for q in range(n // 8):
        left = n - 8 * q
        rest = left - 8
        cols = [jnp.broadcast_to(d[:, 8 * q + k : 8 * q + k + 1], (left, B)) for k in range(8)]
        tops, lows = [], []
        scale = jnp.zeros((8, B), F32)
        for k in range(8):
            pivot = jnp.broadcast_to(cols[k][k : k + 1, :], (8, B))
            reciprocal = 1.0 / pivot
            scale = jnp.where(sub == k, lax.rsqrt(pivot), scale)
            top = jnp.where(sub > k, cols[k][:8] * reciprocal, 0.0)
            tops.append(top)
            if rest:
                low = cols[k][8:] * jnp.broadcast_to(reciprocal[:1], (rest, B))
                lows.append(low)
            for l in range(k + 1, 8):
                u = cols[l][k : k + 1, :]
                t = cols[l][:8] - top * jnp.broadcast_to(u, (8, B))
                if rest:
                    r = cols[l][8:] - low * jnp.broadcast_to(u, (rest, B))
                    t = jnp.concatenate([t, r], 0)
                cols[l] = t
        d_top, e_top = d[:8], e[:8]
        d_rows, e_rows = [], []
        for k in range(8):
            a, b = d_top[k : k + 1, :], e_top[k : k + 1, :]
            d_rows.append(a)
            e_rows.append(b)
            d_top = d_top - tops[k] * jnp.broadcast_to(a, (8, B))
            e_top = e_top - tops[k] * jnp.broadcast_to(b, (8, B))
        out.append(e_top * scale)
        if rest:
            d, e = d[8:], e[8:]
            for k in range(8):
                d = d - lows[k] * jnp.broadcast_to(d_rows[k], (rest, B))
                e = e - lows[k] * jnp.broadcast_to(e_rows[k], (rest, B))
    return jnp.concatenate(out, 0)


VMEM = pl.BlockSpec(memory_space=pltpu.VMEM)
ANY = pl.BlockSpec(memory_space=pl.ANY)
SMEM = pl.BlockSpec(memory_space=pltpu.SMEM)
CHIPS = 16
LEAD = 24


def rows_of(chip, core):
    return pl.ds(pl.multiple_of(16 * chip + 8 * core, 8), 8)


def small(kernel, outs, specs, *args):
    return pl.pallas_call(
        kernel,
        out_shape=[jax.ShapeDtypeStruct(shape, F32) for shape in outs],
        in_specs=specs,
        out_specs=[VMEM] * len(outs),
        compiler_params=pltpu.CompilerParams(vmem_limit_bytes=4 * MIB),
        cost_estimate=pl.CostEstimate(flops=0, bytes_accessed=2 * MIB, transcendentals=0),
    )(*args)


def column_kernel(a, *refs):
    outs, (buf, sem) = refs[:4], refs[4:]
    size = 8 * T
    loads = [pltpu.make_async_copy(a.at[pl.ds(m * size, size)], buf.at[pl.ds(m * size, size)], sem.at[m]) for m in range(4)]
    for load in loads:
        load.start()
    for m in range(4):
        loads[m].wait()
        for half in range(2):
            outs[m][:, half * B : (half + 1) * B] = buf[pl.ds(m * size + half * 4, T, stride=8), :]


def tile_column(a):
    return pl.pallas_call(
        column_kernel,
        out_shape=[square(T)] * 4,
        in_specs=[pl.BlockSpec(memory_space=pltpu.HBM)],
        out_specs=[VMEM] * 4,
        scratch_shapes=[pltpu.VMEM((4 * T * 8, B), F32), pltpu.SemaphoreType.DMA((4,))],
        compiler_params=pltpu.CompilerParams(vmem_limit_bytes=8 * MIB),
        cost_estimate=pl.CostEstimate(flops=0, bytes_accessed=5 * MIB, transcendentals=0),
    )(pltpu.with_memory_space_constraint(a, pltpu.HBM))


def outward_kernel(where, pieces, first, got1, got2, got3, out, share):
    for z in range(8):
        for i, tile in enumerate((z, z + 8, z + 16, z + 24, 0, 1)):
            out[z, 8 * i : 8 * i + 8] = pieces[tile]
    share[...] = jnp.where(where[1] < 2, first[...], got1[...] + got2[...] + got3[...])


def inward_kernel(lines, tile, out, share):
    for j in range(CHIPS):
        out[j, 0:16] = lines[0, 32:48]
        out[j, 16:LEAD] = lines[1, 40:48]
        out[j, LEAD : LEAD + 32] = lines[0, 0:32]
        out[j, LEAD + 32 :] = lines[1, 0:32]
    share[...] = tile[...]


def head_kernel(both, right, left, ready1, ready2, lead, up, down, top, bottom):
    lead[...] = both[:, 0:LEAD]
    up[...] = right[...]
    down[...] = left[...]
    top[...] = right[0:B]
    bottom[...] = left[B:]


def first_kernel(where, mine, other, both, w, e_low, a_low, same, a, e, tiles):
    core = lax.rem(where[0], 2)
    for j in range(CHIPS):
        for t in range(3):
            tiles[t, rows_of(j, core)] = mine[j, 8 * t : 8 * t + 8]
            tiles[t, rows_of(j, 1 - core)] = other[j, 8 * t : 8 * t + 8]
    a[0:T, 0:T] = 0.5 * (tiles[0] + tiles[0].T)
    a[T:, 0:T] = tiles[1]
    a[T:, T:] = 0.5 * (tiles[2] + tiles[2].T)
    w[...] = jnp.zeros_like(w)
    e[...] = jnp.zeros_like(e)
    for i in range(2):
        o = i * B
        p = o + B
        part = leaf(a[o:p, o:p])
        w[o:p, o:p] = part
        if i:
            w[o:p, 0:o] = dot(part, e[o:p, 0:o])
        low = dot_t(a[p:, o:p], part)
        for j in range(i + 1, 4):
            r = (j - i - 1) * B
            a[j * B :, j * B : (j + 1) * B] -= dot_t(low[r:], low[r : r + B])
        e[p:, 0:p] -= dot(low, w[o:p, 0:p])
    e_low[...] = e[T:, :]
    a_low[...] = a[T:, T:]


def second_kernel(a, e_low, w, w_low):
    top = leaf(a[0:B, 0:B])
    low = dot_t(a[B:, 0:B], top)
    end = leaf(a[B:, B:] - dot_t(low, low))
    w[0:B, 0:B] = top
    w[0:B, B:] = jnp.zeros((B, B), F32)
    w[B:, 0:B] = -dot(end, dot(low, top))
    w[B:, B:] = end
    w_low[...] = dot(w[...], e_low[...])


def square(n):
    return jax.ShapeDtypeStruct((n, n), F32)


def first_factor(where, mine, other, both):
    far = pl.BlockSpec(memory_space=pl.ANY)
    return pl.pallas_call(
        first_kernel,
        out_shape=[square(T)] * 3 + [jax.ShapeDtypeStruct(both.shape, F32)],
        in_specs=[SMEM, VMEM, VMEM, far],
        out_specs=[VMEM] * 3 + [far],
        input_output_aliases={3: 3},
        scratch_shapes=[pltpu.VMEM((2 * T, 2 * T), F32), pltpu.VMEM((2 * T, T), F32), pltpu.VMEM((3, T, T), F32)],
        compiler_params=pltpu.CompilerParams(vmem_limit_bytes=12 * MIB),
        cost_estimate=pl.CostEstimate(flops=10**9, bytes_accessed=40 * MIB, transcendentals=0),
    )(where, mine, other, both)


def second_factor(a, e_low):
    return pl.pallas_call(
        second_kernel,
        out_shape=[square(T)] * 2,
        in_specs=[VMEM] * 2,
        out_specs=[VMEM] * 2,
        compiler_params=pltpu.CompilerParams(vmem_limit_bytes=12 * MIB),
        cost_estimate=pl.CostEstimate(flops=10**9, bytes_accessed=40 * MIB, transcendentals=0),
    )(a, e_low)


def split(x):
    high = x.astype(BF16)
    return high, (x - high.astype(F32)).astype(BF16)


def thirds(x):
    high = x.astype(BF16)
    rest = x - high.astype(F32)
    middle = rest.astype(BF16)
    return high, middle, (rest - middle.astype(F32)).astype(BF16)


def mul(u, v):
    return lax.dot_general(u, v, (((1,), (1,)), ((), ())), preferred_element_type=F32)


def lay(ref, at, x, order):
    parts = thirds(x)
    for i, part in enumerate(order):
        ref[:, at + i * T : at + (i + 1) * T] = parts[part]


LEFT = (0, 0, 1, 1, 0, 2)
RIGHT = (0, 1, 0, 1, 2, 0)
SIX = 6 * T
STEP = 256


def update_kernel(where, a, *refs):
    panels, refs = refs[:9], refs[9:]
    mine, other, w00, w10, w11, out, buf, panel, mirror, x_out, left, right, x_cat, y_cat, sem_a, sem_out = refs
    r, c = where[0], where[1]
    core = lax.rem(r, 2)
    n_part = 8 * T
    loads = [pltpu.make_async_copy(a.at[pl.ds(i * n_part, n_part)], buf.at[pl.ds(i * n_part, n_part)], sem_a.at[i]) for i in range(4)]
    for load in loads:
        load.start()
    for i, t in enumerate((w00, w10, w11)):
        lay(right, i * SIX, t[...], RIGHT)

    def solve(first, second, stride, start, cat, order, keep):
        lay(left, 0, first, LEFT)
        lay(left, SIX, second, LEFT)
        for i in range(0, 4 * T, STEP):
            rows = slice(i, i + STEP)
            x0 = mul(left[rows, 0:SIX], right[:, 0:SIX])
            x1 = mul(left[rows], right[:, SIX:])
            if keep:
                x_out[rows] = jnp.where(c == 0, x0, x1)
            tile = (lax.broadcasted_iota(jnp.int32, (STEP, 1), 0) + i) // T * stride + start
            for k, x in enumerate((x0, x1)):
                parts = split(jnp.where(tile > k, x, 0.0))
                for j, part in enumerate(order):
                    at = (2 * j + k) * T
                    cat[rows, at : at + T] = parts[part]

    for j in range(CHIPS):
        for k in range(2):
            for n in range(4):
                at = LEAD + 32 * k + 8 * n
                mirror[k, n, rows_of(j, core)] = mine[j, at : at + 8]
                mirror[k, n, rows_of(j, 1 - core)] = other[j, at : at + 8]
    solve(mirror[0].reshape(4 * T, T), mirror[1].reshape(4 * T, T), 8, c, y_cat, (0, 0, 1), False)
    for j, part in zip((0, 1, 2, 3, 5, 6, 7), panels):
        panel[lax.rem(c - j + 8, 8)] = part[...]
    panel[lax.rem(c + 4, 8), 0:B] = panels[7][...]
    panel[lax.rem(c + 4, 8), B:] = panels[8][...]
    first = jnp.concatenate([panel[0], panel[7], panel[6], panel[5]], axis=0)
    solve(first, panel[1:5].reshape(4 * T, T), 32, r, x_cat, (0, 1, 0), True)

    rows = T
    stores = []
    for i in range(4):
        loads[i].wait()
        span = slice(i * rows, (i + 1) * rows)
        for n in range(4):
            cols = slice(n * T, (n + 1) * T)
            product = mul(x_cat[span], y_cat[cols])
            for half in range(2):
                at = pl.ds(i * n_part + half * 4 + n, rows, stride=8)
                buf[at, :] = buf[at, :] - product[:, half * B : (half + 1) * B]

        @pl.when(c < 2)
        def _():
            row = lax.broadcasted_iota(jnp.int32, (rows, T), 0) + i * rows
            col = lax.broadcasted_iota(jnp.int32, (rows, T), 1)
            tile = row // T * 32 + r
            keep = (tile > c) | ((tile == c) & (lax.rem(row, T) >= col))
            x = jnp.where(keep, x_out[span], 0.0)
            for half in range(2):
                buf[pl.ds(i * n_part + half * 4, rows, stride=8), :] = x[:, half * B : (half + 1) * B]

        at = pl.ds(i * n_part, n_part)
        stores.append(pltpu.make_async_copy(buf.at[at], out.at[at], sem_out.at[i]))
        stores[i].start()
    for store in stores:
        store.wait()


def update(where, a, panels, mine, other, w):
    hbm = pl.BlockSpec(memory_space=pltpu.HBM)
    a = pltpu.with_memory_space_constraint(a, pltpu.HBM)
    return pl.pallas_call(
        update_kernel,
        out_shape=jax.ShapeDtypeStruct(a.shape, F32),
        in_specs=[SMEM, hbm] + [VMEM] * 14,
        out_specs=hbm,
        scratch_shapes=[
            pltpu.VMEM((4 * T * 8, B), F32),
            pltpu.VMEM((8, T, T), F32),
            pltpu.VMEM((2, 4, T, T), F32),
            pltpu.VMEM((4 * T, T), F32),
            pltpu.VMEM((4 * T, 2 * SIX), BF16),
            pltpu.VMEM((T, 3 * SIX), BF16),
            pltpu.VMEM((4 * T, SIX), BF16),
            pltpu.VMEM((4 * T, SIX), BF16),
            pltpu.SemaphoreType.DMA((4,)),
            pltpu.SemaphoreType.DMA((4,)),
        ],
        compiler_params=pltpu.CompilerParams(vmem_limit_bytes=38 * MIB),
        cost_estimate=pl.CostEstimate(flops=8 * 10**9, bytes_accessed=12 * MIB, transcendentals=0),
    )(where, a, *panels, mine, other, *w)


def along(x, step):
    return lax.ppermute(x, "col", [(z, (z + step) % 8) for z in range(8)])


def per_device(matrix):
    r = lax.axis_index("row")
    c = lax.axis_index("col")
    where = jnp.stack([r, c]).astype(jnp.int32)
    flat = matrix.reshape(4, T, 4, 2, B).transpose(0, 1, 3, 2, 4).reshape(4 * T * 8, B)
    column = tile_column(flat)
    first = column[0]
    tile = (T, T)
    half = (B, T)

    got = [lax.ppermute(column[m], "col", [(0, 8 - m), (1, 1 + m)]) for m in (1, 2, 3)]
    pieces = lax.all_to_all(first.reshape(32, 8, T), "row", 0, 0)
    spread, share = small(outward_kernel, [(8, 48, T), tile], [SMEM] + [VMEM] * 5, where, pieces, first, *got)
    lines = lax.all_to_all(spread, "col", 0, 0)
    both, share = small(inward_kernel, [(CHIPS, LEAD + 64, T), tile], [VMEM] * 2, lines, share)
    near = [along(share, step) for step in (1, 2, -2, -1)]

    cores = [[2 * j + k for j in range(CHIPS)] for k in range(2)]
    swap = [(i, i ^ 1) for i in range(32)]
    both = lax.all_to_all(both, "row", 0, 0, axis_index_groups=cores)
    lead, up, down, top, bottom = small(
        head_kernel, [(CHIPS, LEAD, T), tile, tile, half, half], [VMEM] * 3 + [ANY] * 2, both, near[1], near[2], near[0], near[3]
    )
    far = [along(up, 1), along(down, -1), along(top, 2), along(bottom, -2)]
    w00, e_low, a_low, both = first_factor(where, lead, lax.ppermute(lead, "row", swap), both)
    w11, w10 = second_factor(a_low, e_low)
    panels = [share, near[0], near[1], far[0], far[1], near[2], near[3], far[2], far[3]]
    out = update(where, flat, panels, both, lax.ppermute(both, "row", swap), (w00, w10, w11))
    return out.reshape(4, T, 2, 4, B).transpose(0, 1, 3, 2, 4).reshape(4, T, 4, T)


def solution(mesh):
    spec = P(None, "row", None, "col")
    return jax.shard_map(per_device, mesh=mesh, in_specs=(spec,), out_specs=spec, check_vma=False)
```
